256 devices in a mesh: pts: 256 (over z, y, x, core).
Axes of the slice: x: 4, y: 4, z: 8, core: 2. Of those that a mesh axis runs over, the one named last changes fastest.
Arguments:
- points: float32 [64, 524288], P(None, 'pts'), may hold values from -6 to 6
- probes: float32 [32, 524288], P(None, 'pts'), may hold values from -0.078125 to 0.078125
- inv_length: float32 [64], replicated, may hold values from 0.03 to 0.6
- partners: int32 [2, 256], replicated, may hold values from 0 to 255, as said below
Outputs:
- product: float32 [32, 524288], P(None, 'pts')
The draws below stay inside these ranges and needn't reach their ends.
Inputs may be any that keep to these rules, and one draw needn't show every extreme that they name: partners[r, i] = i XOR m_r, with masks m_r of 1 to 255 that differ between rounds; so every round pairs the blocks two by two.
All inputs are finite; a program needn't handle non-finite values.
Results may differ from the reference program's by a relative error of at most 0.0003.
Values sent between devices are 32-bit elements; how exact they have to be, the bound alone decides.
A program may use at most 64 MiB of HBM per device.

```python
import math
import jax
import jax.numpy as jnp
from jax import lax

FEAT = 64
PROBES = 32
BLK = 2048
ROUNDS = 2
POINTS = 524288
N_PTS = 256


def draw_partners(key, part):
    key = jax.random.fold_in(key, 11)
    order = jax.random.permutation(key, N_PTS - 1).astype(jnp.int32) + 1
    masks = order[:ROUNDS].astype(jnp.int32)
    blocks = jnp.arange(N_PTS, dtype=jnp.int32)
    return jnp.bitwise_xor(blocks[None, :], masks[:, None]).astype(jnp.int32)


def level_of(rng, dims, cuts, least, high):
    def one(axis_at, parts):
        draws = jax.random.uniform(jax.random.fold_in(jax.random.fold_in(rng, 6), axis_at), (parts,), jnp.float32, least / len(cuts), high / len(cuts))
        return jnp.repeat(jnp.exp(draws), dims[axis_at] // parts).reshape((-1,) + (1,) * (len(dims) - axis_at - 1))

    factor_of = one(*cuts[0])
    for cut in cuts[1:]:
        factor_of = factor_of * one(*cut)
    return factor_of


def noise(own_key, extent, deviation, reach, shards=(), kind=jnp.bfloat16):
    entries = deviation * jax.random.normal(own_key, extent, jnp.float32)
    if shards:
        entries = entries * level_of(own_key, extent, shards, -0.22, 0.18)
    return jnp.clip(entries, -reach, reach).astype(kind)


def setup_inputs(seed: int = 0) -> dict:
    streams_of = jax.random.split(jax.random.key(seed), 5)
    points = noise(streams_of[0], (FEAT, POINTS), 1.0, 6.0, ((1, 256),), jnp.float32)
    probes = noise(streams_of[1], (PROBES, POINTS), (3 * BLK) ** -0.5, 0.078125, ((1, 256),), jnp.float32)
    inv_length = jnp.clip(jnp.exp(jax.random.uniform(streams_of[2], (FEAT,), jnp.float32, math.log(0.03), math.log(0.6))), 0.03, 0.6)
    partners = draw_partners(jax.random.fold_in(streams_of[4], 71), 0)
    return dict(points=points, probes=probes, inv_length=inv_length, partners=partners)


root_five = 5.0 ** 0.5

def matern(left, right):
    inner = lax.dot_general(left, right, (((0,), (0,)), ((), ())), precision=lax.Precision.HIGHEST, preferred_element_type=jnp.float32)
    left_sq = lax.optimization_barrier(jnp.sum(left * left, axis=0))
    right_sq = lax.optimization_barrier(jnp.sum(right * right, axis=0))
    dist_sq = jnp.maximum(left_sq[:, None] + right_sq[None, :] - 2.0 * inner, 0.0)
    scaled_dist = root_five * jnp.sqrt(dist_sq)
    return (1.0 + scaled_dist + scaled_dist * scaled_dist / 3.0) * jnp.exp(-scaled_dist)

def block_terms(left, right, weights):
    rows = left.shape[1]
    step = min(256, rows)
    pieces = left.reshape(left.shape[0], rows // step, step).transpose(1, 0, 2)

    def one_piece(piece):
        kernel = matern(piece, right)
        return lax.dot_general(weights, kernel, (((1,), (1,)), ((), ())), precision=lax.Precision.HIGHEST, preferred_element_type=jnp.float32)
    outs = lax.map(one_piece, pieces)
    return outs.transpose(1, 0, 2).reshape(weights.shape[0], rows)

def reference(points, probes, inv_length, partners):
    scaled = points * inv_length[:, None]
    count = partners.shape[1]

    def one_block(block):
        start = (block * BLK).astype(jnp.int32)
        own = lax.dynamic_slice_in_dim(scaled, start, BLK, 1)
        total = block_terms(own, own, lax.dynamic_slice_in_dim(probes, start, BLK, 1))
        for round_index in range(ROUNDS):
            other = partners[round_index, block].astype(jnp.int32)
            other_start = (other * BLK).astype(jnp.int32)
            far = lax.dynamic_slice_in_dim(scaled, other_start, BLK, 1)
            far_probes = lax.dynamic_slice_in_dim(probes, other_start, BLK, 1)
            total = total + block_terms(own, far, far_probes)
        return total
    result = lax.map(one_block, jnp.arange(count, dtype=jnp.int32))
    return result.transpose(1, 0, 2).reshape(probes.shape[0], count * BLK)
```

```python
import math

import jax
import jax.experimental.pallas as pl
import jax.experimental.pallas.tpu as pltpu
import jax.numpy as jnp
from jax import lax
from jax.sharding import PartitionSpec as P

N = 256
FEAT = 64
PROBES = 32
BLK = 2048
ROUNDS = 2
ROWS = 6
GROUPS = (FEAT + PROBES) // ROWS
MESH = pl.DeviceIdType.MESH

LN2 = math.log(2.0)
COORD = math.sqrt(5.0) / LN2
ALPHA = 3.0 / LN2
BETA = 3.0 / LN2**2
GAMMA = LN2**2 / 3.0

TP = 2048
TQ = 256
f32 = jnp.float32
bf16 = jnp.bfloat16


def split(x):
    high = x.astype(bf16)
    return high, (x - high.astype(f32)).astype(bf16)


def set_right(cat, right, right_sq, weights):
    high, low = split(cat[:FEAT, :])
    rounded = high.astype(f32) + low.astype(f32)
    right[...] = jnp.concatenate([high, low, high, low], 0)
    right_sq[...] = jnp.sum(rounded * rounded, axis=0, keepdims=True)
    high, low = split(cat[FEAT:, :])
    weights[...] = jnp.concatenate([high, low], 0)


def set_left(cat, left, left_sq):
    high, low = split(cat[:FEAT, :].T)
    rounded = high.astype(f32) + low.astype(f32)
    left_sq[...] = jnp.sum(rounded * rounded, axis=1, keepdims=True)
    high, low = high * bf16(-2), low * bf16(-2)
    left[...] = jnp.concatenate([high, high, low, low], 1)


def add_block(left, left_sq, right, right_sq, weights, total):
    n_p = BLK // TP

    def step(i, carry):
        ps = pl.ds(pl.multiple_of(lax.rem(i, n_p) * TP, TP), TP)
        qs = pl.ds(pl.multiple_of((i // n_p) * TQ, TQ), TQ)
        inner = jnp.dot(left[ps, :], right[:, qs], preferred_element_type=f32)
        d = jnp.maximum((inner + left_sq[ps, :]) + right_sq[:, qs], 1e-30)
        t = d * lax.rsqrt(d)
        k = ((d + BETA) + ALPHA * t) * jnp.exp2(-t)
        high, low = split(k)
        w = weights[:, qs]
        dims = (((1,), (1,)), ((), ()))
        total[ps, :] += lax.dot_general(high, w, dims, preferred_element_type=f32) + lax.dot_general(
            low, w, dims, preferred_element_type=f32
        )
        return carry

    lax.fori_loop(0, n_p * (BLK // TQ), step, 0)


def kernel(
    partners, points, probes, inv_length, out,
    cat, stage, mid, send, recv, left, left_sq, right, right_sq, weights, total,
    spread_send, spread_recv, deliver_send, deliver_recv,
):
    me = lax.axis_index("pts")

    def target(d):
        return lax.rem(me + lax.rem(d, 8) * 32 + d // 8, N)

    barrier = pltpu.get_barrier_semaphore()

    @pl.loop(1, N)
    def _(d):
        pl.semaphore_signal(barrier, inc=1, device_id=(target(d),), device_id_type=MESH)

    cat[:FEAT, :] = points[...] * (inv_length[...] * COORD)
    cat[FEAT:, :] = probes[...]

    @pl.loop(0, BLK // 128)
    def _(c):
        columns = pl.ds(pl.multiple_of(c * 128, 128), 128)
        for g in range(GROUPS):
            stage[c * GROUPS + g] = cat[g * ROWS : (g + 1) * ROWS, columns]

    pl.semaphore_wait(barrier, N - 1)

    @pl.loop(1, N)
    def _(d):
        t = target(d)
        pltpu.make_async_remote_copy(
            src_ref=stage.at[t], dst_ref=mid.at[me], send_sem=spread_send, recv_sem=spread_recv,
            device_id=(t,), device_id_type=MESH,
        ).start()

    mid[me] = stage[me]

    total[...] = jnp.zeros_like(total)
    set_right(cat, right, right_sq, weights)
    set_left(cat, left, left_sq)
    add_block(left, left_sq, right, right_sq, weights, total)

    most = pl.ds(0, N - 1)
    pltpu.make_async_copy(mid.at[most], mid.at[most], spread_recv).wait()

    for r in range(ROUNDS):

        @pl.loop(1, N)
        def _(d):
            t = target(d)
            send[r, t] = mid[partners[r, t]]
            pltpu.make_async_remote_copy(
                src_ref=send.at[r, t], dst_ref=recv.at[r, me], send_sem=deliver_send.at[r],
                recv_sem=deliver_recv.at[r], device_id=(t,), device_id_type=MESH,
            ).start()

        recv[r, me] = mid[partners[r, me]]

    for r in range(ROUNDS):
        pltpu.make_async_copy(recv.at[r, most], recv.at[r, most], deliver_recv.at[r]).wait()

        @pl.loop(0, BLK // 128)
        def _(c):
            columns = pl.ds(pl.multiple_of(c * 128, 128), 128)
            for g in range(GROUPS):
                cat[g * ROWS : (g + 1) * ROWS, columns] = recv[r, c * GROUPS + g]

        set_right(cat, right, right_sq, weights)
        add_block(left, left_sq, right, right_sq, weights, total)

    pltpu.make_async_copy(stage.at[most], stage.at[most], spread_send).wait()
    for r in range(ROUNDS):
        pltpu.make_async_copy(send.at[r, most], send.at[r, most], deliver_send.at[r]).wait()
    sums = total[...]
    out[...] = ((sums[:, :PROBES] + sums[:, PROBES:]) * GAMMA).T


def body(points, probes, inv_length, partners):
    vmem = pl.BlockSpec(memory_space=pltpu.VMEM)
    return pl.pallas_call(
        kernel,
        out_shape=jax.ShapeDtypeStruct((PROBES, BLK), f32),
        in_specs=[pl.BlockSpec(memory_space=pltpu.SMEM), vmem, vmem, vmem],
        out_specs=vmem,
        scratch_shapes=[
            pltpu.VMEM((FEAT + PROBES, BLK), f32),
            pltpu.VMEM((N, ROWS, 128), f32),
            pltpu.VMEM((N, ROWS, 128), f32),
            pltpu.VMEM((ROUNDS, N, ROWS, 128), f32),
            pltpu.VMEM((ROUNDS, N, ROWS, 128), f32),
            pltpu.VMEM((BLK, 4 * FEAT), bf16),
            pltpu.VMEM((BLK, 1), f32),
            pltpu.VMEM((4 * FEAT, BLK), bf16),
            pltpu.VMEM((1, BLK), f32),
            pltpu.VMEM((2 * PROBES, BLK), bf16),
            pltpu.VMEM((BLK, 2 * PROBES), f32),
            pltpu.SemaphoreType.DMA,
            pltpu.SemaphoreType.DMA,
            pltpu.SemaphoreType.DMA((ROUNDS,)),
            pltpu.SemaphoreType.DMA((ROUNDS,)),
        ],
        compiler_params=pltpu.CompilerParams(collective_id=0, has_side_effects=True, vmem_limit_bytes=48 << 20),
    )(partners, points, probes, inv_length[:, None])


def solution(mesh):
    in_specs = (P(None, "pts"), P(None, "pts"), P(), P())
    return jax.shard_map(body, mesh=mesh, in_specs=in_specs, out_specs=P(None, "pts"), check_vma=False)
```

```python
import math

import jax
import jax.experimental.pallas as pl
import jax.experimental.pallas.tpu as pltpu
import jax.numpy as jnp
from jax import lax
from jax.sharding import PartitionSpec as P

N = 256
FEAT = 64
PROBES = 32
BLK = 2048
ROUNDS = 2
ROWS = 6
GROUPS = (FEAT + PROBES) // ROWS
MESH = pl.DeviceIdType.MESH

LN2 = math.log(2.0)
COORD = math.sqrt(5.0) / LN2
ALPHA = 3.0 / LN2
BETA = 3.0 / LN2**2
GAMMA = LN2**2 / 3.0

PARTS = 2
TQ = 256
f32 = jnp.float32
bf16 = jnp.bfloat16


def split(x):
    high = x.astype(bf16)
    return high, (x - high.astype(f32)).astype(bf16)


def set_right(cat, right, right_sq, weights):
    high, low = split(cat[:FEAT, :])
    rounded = high.astype(f32) + low.astype(f32)
    right[...] = jnp.concatenate([high, low, high, low], 0)
    right_sq[...] = jnp.sum(rounded * rounded, axis=0, keepdims=True)
    high, low = split(cat[FEAT:, :])
    weights[...] = jnp.concatenate([high, low], 0)


def set_left(cat, left, left_sq):
    high, low = split(cat[:FEAT, :].T)
    rounded = high.astype(f32) + low.astype(f32)
    left_sq[...] = jnp.sum(rounded * rounded, axis=1, keepdims=True)
    high, low = high * bf16(-2), low * bf16(-2)
    left[...] = jnp.concatenate([high, high, low, low], 1)


def add_block(left, left_sq, right, right_sq, weights, total):
    dims = (((1,), (1,)), ((), ()))

    def step(i, carry):
        sums = None
        for part in range(PARTS):
            qs = pl.ds(pl.multiple_of((i * PARTS + part) * TQ, TQ), TQ)
            inner = jnp.dot(left[...], right[:, qs], preferred_element_type=f32)
            d = jnp.maximum((inner + left_sq[...]) + right_sq[:, qs], 1e-30)
            t = d * lax.rsqrt(d)
            k = ((d + BETA) + ALPHA * t) * jnp.exp2(-t)
            high, low = split(k)
            w = weights[:, qs]
            term = lax.dot_general(high, w, dims, preferred_element_type=f32) + lax.dot_general(
                low, w, dims, preferred_element_type=f32
            )
            sums = term if sums is None else sums + term
        total[...] += sums
        return carry

    lax.fori_loop(0, BLK // (PARTS * TQ), step, 0)


def kernel(
    partners, points, probes, inv_length, out,
    cat, stage, mid, send, recv, left, left_sq, right, right_sq, weights, total,
    spread_send, spread_recv, deliver_send, deliver_recv,
):
    me = lax.axis_index("pts")

    def target(d):
        return lax.rem(me + lax.rem(d, 8) * 32 + d // 8, N)

    barrier = pltpu.get_barrier_semaphore()

    @pl.loop(1, N)
    def _(d):
        pl.semaphore_signal(barrier, inc=1, device_id=(target(d),), device_id_type=MESH)

    scale = jnp.broadcast_to(inv_length[...] * COORD, (8, FEAT)).T[:, :1]
    cat[:FEAT, :] = points[...] * scale
    cat[FEAT:, :] = probes[...]

    @pl.loop(0, BLK // 128)
    def _(c):
        columns = pl.ds(pl.multiple_of(c * 128, 128), 128)
        for g in range(GROUPS):
            stage[c * GROUPS + g] = cat[g * ROWS : (g + 1) * ROWS, columns]

    pl.semaphore_wait(barrier, N - 1)

    @pl.loop(1, N)
    def _(d):
        t = target(d)
        pltpu.make_async_remote_copy(
            src_ref=stage.at[t], dst_ref=mid.at[me], send_sem=spread_send, recv_sem=spread_recv,
            device_id=(t,), device_id_type=MESH,
        ).start()

    mid[me] = stage[me]

    total[...] = jnp.zeros_like(total)
    set_right(cat, right, right_sq, weights)
    set_left(cat, left, left_sq)
    add_block(left, left_sq, right, right_sq, weights, total)

    most = pl.ds(0, N - 1)
    pltpu.make_async_copy(mid.at[most], mid.at[most], spread_recv).wait()

    for r in range(ROUNDS):

        @pl.loop(1, N)
        def _(d):
            t = target(d)
            send[r, t] = mid[partners[r, t]]
            pltpu.make_async_remote_copy(
                src_ref=send.at[r, t], dst_ref=recv.at[r, me], send_sem=deliver_send.at[r],
                recv_sem=deliver_recv.at[r], device_id=(t,), device_id_type=MESH,
            ).start()

        recv[r, me] = mid[partners[r, me]]

    for r in range(ROUNDS):
        pltpu.make_async_copy(recv.at[r, most], recv.at[r, most], deliver_recv.at[r]).wait()

        @pl.loop(0, BLK // 128)
        def _(c):
            columns = pl.ds(pl.multiple_of(c * 128, 128), 128)
            for g in range(GROUPS):
                cat[g * ROWS : (g + 1) * ROWS, columns] = recv[r, c * GROUPS + g]

        set_right(cat, right, right_sq, weights)
        add_block(left, left_sq, right, right_sq, weights, total)

    pltpu.make_async_copy(stage.at[most], stage.at[most], spread_send).wait()
    for r in range(ROUNDS):
        pltpu.make_async_copy(send.at[r, most], send.at[r, most], deliver_send.at[r]).wait()
    sums = total[...]
    out[...] = ((sums[:, :PROBES] + sums[:, PROBES:]) * GAMMA).T


def body(points, probes, inv_length, partners):
    vmem = pl.BlockSpec(memory_space=pltpu.VMEM)
    return pl.pallas_call(
        kernel,
        out_shape=jax.ShapeDtypeStruct((PROBES, BLK), f32),
        in_specs=[pl.BlockSpec(memory_space=pltpu.SMEM), vmem, vmem, vmem],
        out_specs=vmem,
        scratch_shapes=[
            pltpu.VMEM((FEAT + PROBES, BLK), f32),
            pltpu.VMEM((N, ROWS, 128), f32),
            pltpu.VMEM((N, ROWS, 128), f32),
            pltpu.VMEM((ROUNDS, N, ROWS, 128), f32),
            pltpu.VMEM((ROUNDS, N, ROWS, 128), f32),
            pltpu.VMEM((BLK, 4 * FEAT), bf16),
            pltpu.VMEM((BLK, 1), f32),
            pltpu.VMEM((4 * FEAT, BLK), bf16),
            pltpu.VMEM((1, BLK), f32),
            pltpu.VMEM((2 * PROBES, BLK), bf16),
            pltpu.VMEM((BLK, 2 * PROBES), f32),
            pltpu.SemaphoreType.DMA,
            pltpu.SemaphoreType.DMA,
            pltpu.SemaphoreType.DMA((ROUNDS,)),
            pltpu.SemaphoreType.DMA((ROUNDS,)),
        ],
        compiler_params=pltpu.CompilerParams(collective_id=0, has_side_effects=True, vmem_limit_bytes=62 << 20),
    )(partners, points, probes, inv_length[None, :])


def solution(mesh):
    in_specs = (P(None, "pts"), P(None, "pts"), P(), P())
    return jax.shard_map(body, mesh=mesh, in_specs=in_specs, out_specs=P(None, "pts"), check_vma=False)
```

```python
import math

import jax
import jax.experimental.pallas as pl
import jax.experimental.pallas.tpu as pltpu
import jax.numpy as jnp
from jax import lax
from jax.sharding import PartitionSpec as P

N = 256
FEAT = 64
PROBES = 32
BLK = 2048
ROUNDS = 2
ROWS = 6
GROUPS = (FEAT + PROBES) // ROWS
MESH = pl.DeviceIdType.MESH

LN2 = math.log(2.0)
COORD = math.sqrt(5.0) / LN2
ALPHA = 3.0 / LN2
BETA = 3.0 / LN2**2
GAMMA = LN2**2 / 3.0

PARTS = 4
TQ = 256
f32 = jnp.float32
bf16 = jnp.bfloat16


def split(x):
    high = x.astype(bf16)
    return high, (x - high.astype(f32)).astype(bf16)


def set_right(cat, right, right_sq, weights):
    high, low = split(cat[:FEAT, :])
    rounded = high.astype(f32) + low.astype(f32)
    right[...] = jnp.concatenate([high, low, high, low], 0)
    right_sq[...] = jnp.sum(rounded * rounded, axis=0, keepdims=True)
    high, low = split(cat[FEAT:, :])
    weights[...] = jnp.concatenate([high, low], 0)


def set_left(cat, left, left_sq):
    high, low = split(cat[:FEAT, :].T)
    rounded = high.astype(f32) + low.astype(f32)
    left_sq[...] = jnp.sum(rounded * rounded, axis=1, keepdims=True)
    high, low = high * bf16(-2), low * bf16(-2)
    left[...] = jnp.concatenate([high, high, low, low], 1)


def add_block(left, left_sq, right, right_sq, weights, total):
    dims = (((1,), (1,)), ((), ()))

    def step(i, carry):
        sums = None
        for part in range(PARTS):
            qs = pl.ds(pl.multiple_of((i * PARTS + part) * TQ, TQ), TQ)
            inner = jnp.dot(left[...], right[:, qs], preferred_element_type=f32)
            d = jnp.maximum((inner + left_sq[...]) + right_sq[:, qs], 1e-30)
            t = d * lax.rsqrt(d)
            k = ((d + BETA) + ALPHA * t) * jnp.exp2(-t)
            high, low = split(k)
            w = weights[:, qs]
            term = lax.dot_general(high, w, dims, preferred_element_type=f32) + lax.dot_general(
                low, w, dims, preferred_element_type=f32
            )
            sums = term if sums is None else sums + term
        total[...] += sums
        return carry

    lax.fori_loop(0, BLK // (PARTS * TQ), step, 0)


def kernel(
    partners, points, probes, inv_length, out,
    cat, stage, mid, send, recv, left, left_sq, right, right_sq, weights, total,
    spread_send, spread_recv, deliver_send, deliver_recv,
):
    me = lax.axis_index("pts")

    def target(d):
        return lax.rem(me + lax.rem(d, 8) * 32 + d // 8, N)

    barrier = pltpu.get_barrier_semaphore()
    scale = jnp.broadcast_to(inv_length[...] * COORD, (8, FEAT)).T[:, :1]
    cat[:FEAT, :] = points[...] * scale
    cat[FEAT:, :] = probes[...]

    def put(c):
        columns = pl.ds(pl.multiple_of(c * 128, 128), 128)
        for g in range(GROUPS):
            stage[c * GROUPS + g] = cat[g * ROWS : (g + 1) * ROWS, columns]

    @pl.loop(0, 15)
    def _(c):
        for g in range(17):
            t = lax.rem(me + (c * 17 + g + 1), N)
            pl.semaphore_signal(barrier, inc=1, device_id=(t,), device_id_type=MESH)
        put(c)

    put(15)

    pl.semaphore_wait(barrier, N - 1)

    @pl.loop(1, N)
    def _(d):
        t = target(d)
        pltpu.make_async_remote_copy(
            src_ref=stage.at[t], dst_ref=mid.at[me], send_sem=spread_send, recv_sem=spread_recv,
            device_id=(t,), device_id_type=MESH,
        ).start()

    mid[me] = stage[me]

    total[...] = jnp.zeros_like(total)
    set_right(cat, right, right_sq, weights)
    set_left(cat, left, left_sq)
    add_block(left, left_sq, right, right_sq, weights, total)

    most = pl.ds(0, N - 1)
    pltpu.make_async_copy(mid.at[most], mid.at[most], spread_recv).wait()

    for r in range(ROUNDS):

        @pl.loop(1, N)
        def _(d):
            t = target(d)
            send[r, t] = mid[partners[r, t]]
            pltpu.make_async_remote_copy(
                src_ref=send.at[r, t], dst_ref=recv.at[r, me], send_sem=deliver_send.at[r],
                recv_sem=deliver_recv.at[r], device_id=(t,), device_id_type=MESH,
            ).start()

        recv[r, me] = mid[partners[r, me]]

    for r in range(ROUNDS):
        pltpu.make_async_copy(recv.at[r, most], recv.at[r, most], deliver_recv.at[r]).wait()

        @pl.loop(0, BLK // 128)
        def _(c):
            columns = pl.ds(pl.multiple_of(c * 128, 128), 128)
            for g in range(GROUPS):
                cat[g * ROWS : (g + 1) * ROWS, columns] = recv[r, c * GROUPS + g]

        set_right(cat, right, right_sq, weights)
        add_block(left, left_sq, right, right_sq, weights, total)

    pltpu.make_async_copy(stage.at[most], stage.at[most], spread_send).wait()
    for r in range(ROUNDS):
        pltpu.make_async_copy(send.at[r, most], send.at[r, most], deliver_send.at[r]).wait()
    sums = total[...]
    out[...] = ((sums[:, :PROBES] + sums[:, PROBES:]) * GAMMA).T


def body(points, probes, inv_length, partners):
    vmem = pl.BlockSpec(memory_space=pltpu.VMEM)
    return pl.pallas_call(
        kernel,
        out_shape=jax.ShapeDtypeStruct((PROBES, BLK), f32),
        in_specs=[pl.BlockSpec(memory_space=pltpu.SMEM), vmem, vmem, vmem],
        out_specs=vmem,
        scratch_shapes=[
            pltpu.VMEM((FEAT + PROBES, BLK), f32),
            pltpu.VMEM((N, ROWS, 128), f32),
            pltpu.VMEM((N, ROWS, 128), f32),
            pltpu.VMEM((ROUNDS, N, ROWS, 128), f32),
            pltpu.VMEM((ROUNDS, N, ROWS, 128), f32),
            pltpu.VMEM((BLK, 4 * FEAT), bf16),
            pltpu.VMEM((BLK, 1), f32),
            pltpu.VMEM((4 * FEAT, BLK), bf16),
            pltpu.VMEM((1, BLK), f32),
            pltpu.VMEM((2 * PROBES, BLK), bf16),
            pltpu.VMEM((BLK, 2 * PROBES), f32),
            pltpu.SemaphoreType.DMA,
            pltpu.SemaphoreType.DMA,
            pltpu.SemaphoreType.DMA((ROUNDS,)),
            pltpu.SemaphoreType.DMA((ROUNDS,)),
        ],
        compiler_params=pltpu.CompilerParams(collective_id=0, has_side_effects=True, vmem_limit_bytes=60 << 20),
    )(partners, points, probes, inv_length[None, :])


def solution(mesh):
    in_specs = (P(None, "pts"), P(None, "pts"), P(), P())
    return jax.shard_map(body, mesh=mesh, in_specs=in_specs, out_specs=P(None, "pts"), check_vma=False)
```

```python
import math

import jax
import jax.experimental.pallas as pl
import jax.experimental.pallas.tpu as pltpu
import jax.numpy as jnp
from jax import lax
from jax.sharding import PartitionSpec as P

N = 256
FEAT = 64
PROBES = 32
BLK = 2048
HALVES = 2
HALF = BLK // HALVES
ROWS = 3
GROUPS = (FEAT + PROBES) // ROWS
MESH = pl.DeviceIdType.MESH

LN2 = math.log(2.0)
COORD = math.sqrt(5.0) / LN2
ALPHA = 3.0 / LN2
BETA = 3.0 / LN2**2
GAMMA = LN2**2 / 3.0

TQ = 256
f32 = jnp.float32
bf16 = jnp.bfloat16


def split(x):
    high = x.astype(bf16)
    return high, (x - high.astype(f32)).astype(bf16)


def set_left(block, left, left_sq):
    high, low = split(block[:FEAT, :].T)
    rounded = high.astype(f32) + low.astype(f32)
    left_sq[...] = jnp.sum(rounded * rounded, axis=1, keepdims=True)
    high, low = high * bf16(-2), low * bf16(-2)
    left[...] = jnp.concatenate([high, high, low, low], 1)


def add_half(block, left, left_sq, right, right_sq, weights, total):
    high, low = split(block[:FEAT, :])
    rounded = high.astype(f32) + low.astype(f32)
    right[...] = jnp.concatenate([high, low, high, low], 0)
    right_sq[...] = jnp.sum(rounded * rounded, axis=0, keepdims=True)
    high, low = split(block[FEAT:, :])
    weights[...] = jnp.concatenate([high, low], 0)

    dims = (((1,), (1,)), ((), ()))
    sums = None
    for part in range(HALF // TQ):
        qs = pl.ds(part * TQ, TQ)
        inner = jnp.dot(left[...], right[:, qs], preferred_element_type=f32)
        d = jnp.maximum((inner + left_sq[...]) + right_sq[:, qs], 1e-30)
        t = d * lax.rsqrt(d)
        k = ((d + BETA) + ALPHA * t) * jnp.exp2(-t)
        high, low = split(k)
        w = weights[:, qs]
        term = lax.dot_general(high, w, dims, preferred_element_type=f32) + lax.dot_general(
            low, w, dims, preferred_element_type=f32
        )
        sums = term if sums is None else sums + term
    total[...] += sums


def kernel(
    partners, points, probes, inv_length, out,
    own, far, stage, mid, send0, recv0, send1, recv1, left, left_sq, right, right_sq, weights, total,
    spread_send, spread_recv, send0_sem, recv0_sem, send1_sem, recv1_sem,
):
    me = lax.axis_index("pts")
    operands = (left, left_sq, right, right_sq, weights, total)

    def target(d):
        return lax.rem(me + lax.rem(d, 8) * 32 + d // 8, N)

    barrier = pltpu.get_barrier_semaphore()
    scale = jnp.broadcast_to(inv_length[...] * COORD, (8, FEAT)).T[:, :1]
    for h in range(HALVES):
        own[h, :FEAT] = points[:, h * HALF : (h + 1) * HALF] * scale
        own[h, FEAT:] = probes[:, h * HALF : (h + 1) * HALF]

    def put(c, h):
        columns = pl.ds(pl.multiple_of(c * 128, 128), 128)
        for g in range(GROUPS):
            stage[c * GROUPS + g, h] = own[h, g * ROWS : (g + 1) * ROWS, columns]

    @pl.loop(0, 15)
    def _(i):
        for g in range(17):
            t = lax.rem(me + (i * 17 + g + 1), N)
            pl.semaphore_signal(barrier, inc=1, device_id=(t,), device_id_type=MESH)
        put(i // 2, lax.rem(i, 2))

    put(7, 1)

    pl.semaphore_wait(barrier, N - 1)

    @pl.loop(1, N)
    def _(d):
        t = target(d)
        pltpu.make_async_remote_copy(
            src_ref=stage.at[t], dst_ref=mid.at[me], send_sem=spread_send, recv_sem=spread_recv,
            device_id=(t,), device_id_type=MESH,
        ).start()

    mid[me] = stage[me]

    total[...] = jnp.zeros_like(total)
    for h in range(HALVES):
        rows = pl.ds(h * HALF, HALF)
        set_left(own.at[h], left.at[rows], left_sq.at[rows])

    @pl.loop(0, HALVES)
    def _(h):
        add_half(own.at[h], *operands)

    most = pl.ds(0, N - 1)
    pltpu.make_async_copy(mid.at[most], mid.at[most], spread_recv).wait()

    @pl.loop(1, N)
    def _(d):
        t = target(d)
        send0[t] = mid[partners[0, t]]
        pltpu.make_async_remote_copy(
            src_ref=send0.at[t], dst_ref=recv0.at[me], send_sem=send0_sem, recv_sem=recv0_sem,
            device_id=(t,), device_id_type=MESH,
        ).start()

    recv0[me] = mid[partners[0, me]]

    @pl.loop(0, HALVES)
    def _(h):
        @pl.loop(1, N)
        def _(d):
            t = target(d)
            send1[h, t] = mid[partners[1, t], h]
            pltpu.make_async_remote_copy(
                src_ref=send1.at[h, t], dst_ref=recv1.at[h, me], send_sem=send1_sem.at[h], recv_sem=recv1_sem.at[h],
                device_id=(t,), device_id_type=MESH,
            ).start()

        recv1[h, me] = mid[partners[1, me], h]

    pltpu.make_async_copy(recv0.at[most], recv0.at[most], recv0_sem).wait()

    @pl.loop(0, HALVES)
    def _(h):
        @pl.loop(0, HALF // 128)
        def _(c):
            columns = pl.ds(pl.multiple_of(c * 128, 128), 128)
            for g in range(GROUPS):
                far[g * ROWS : (g + 1) * ROWS, columns] = recv0[c * GROUPS + g, h]

        add_half(far, *operands)

    @pl.loop(0, HALVES)
    def _(h):
        pltpu.make_async_copy(recv1.at[h, most], recv1.at[h, most], recv1_sem.at[h]).wait()

        @pl.loop(0, HALF // 128)
        def _(c):
            columns = pl.ds(pl.multiple_of(c * 128, 128), 128)
            for g in range(GROUPS):
                far[g * ROWS : (g + 1) * ROWS, columns] = recv1[h, c * GROUPS + g]

        add_half(far, *operands)

    pltpu.make_async_copy(stage.at[most], stage.at[most], spread_send).wait()
    pltpu.make_async_copy(send0.at[most], send0.at[most], send0_sem).wait()
    for h in range(HALVES):
        pltpu.make_async_copy(send1.at[h, most], send1.at[h, most], send1_sem.at[h]).wait()
    sums = total[...]
    out[...] = ((sums[:, :PROBES] + sums[:, PROBES:]) * GAMMA).T


def body(points, probes, inv_length, partners):
    vmem = pl.BlockSpec(memory_space=pltpu.VMEM)
    return pl.pallas_call(
        kernel,
        out_shape=jax.ShapeDtypeStruct((PROBES, BLK), f32),
        in_specs=[pl.BlockSpec(memory_space=pltpu.SMEM), vmem, vmem, vmem],
        out_specs=vmem,
        scratch_shapes=[
            pltpu.VMEM((HALVES, FEAT + PROBES, HALF), f32),
            pltpu.VMEM((FEAT + PROBES, HALF), f32),
            pltpu.VMEM((N, HALVES, ROWS, 128), f32),
            pltpu.VMEM((N, HALVES, ROWS, 128), f32),
            pltpu.VMEM((N, HALVES, ROWS, 128), f32),
            pltpu.VMEM((N, HALVES, ROWS, 128), f32),
            pltpu.VMEM((HALVES, N, ROWS, 128), f32),
            pltpu.VMEM((HALVES, N, ROWS, 128), f32),
            pltpu.VMEM((BLK, 4 * FEAT), bf16),
            pltpu.VMEM((BLK, 1), f32),
            pltpu.VMEM((4 * FEAT, HALF), bf16),
            pltpu.VMEM((1, HALF), f32),
            pltpu.VMEM((2 * PROBES, HALF), bf16),
            pltpu.VMEM((BLK, 2 * PROBES), f32),
            pltpu.SemaphoreType.DMA,
            pltpu.SemaphoreType.DMA,
            pltpu.SemaphoreType.DMA,
            pltpu.SemaphoreType.DMA,
            pltpu.SemaphoreType.DMA((HALVES,)),
            pltpu.SemaphoreType.DMA((HALVES,)),
        ],
        compiler_params=pltpu.CompilerParams(collective_id=0, has_side_effects=True, vmem_limit_bytes=60 << 20),
    )(partners, points, probes, inv_length[None, :])


def solution(mesh):
    in_specs = (P(None, "pts"), P(None, "pts"), P(), P())
    return jax.shard_map(body, mesh=mesh, in_specs=in_specs, out_specs=P(None, "pts"), check_vma=False)
```
